256 devices in a mesh: tile: 32 (over x_lo, z, core), lev: 8 (over x_hi, y).
Axes of the slice: x: 4 (x_hi: 2, x_lo: 2; x = x_hi * 2 + x_lo), y: 4, z: 8, core: 2. Of those that a mesh axis runs over, the one named last changes fastest.
Arguments:
- gradient: float32 [144, 2, 512, 640], P('lev', None, 'tile'), may hold values from -6 to 6
- land_sea: int32 [144, 512, 640], P('lev', 'tile'), may hold values 0 or 1
- roughness: float32 [144, 512, 640], P('lev', 'tile'), may hold values from 0.5 to 1.4
- scale_index: int32 [10, 144], replicated, may hold values from 0 to 7
- scale_table: float32 [8], replicated, may hold values from 0.03 to 0.12
- balance: float32 [144, 144], replicated, may hold values from -0.5 to 0.5
- corr_a: float32 [144, 144], replicated, may hold values from -0.5 to 0.5
- corr_b: float32 [144, 144], replicated, may hold values from -0.5 to 0.5
Outputs:
- control_grad: float32 [144, 2, 512, 640], P('lev', None, 'tile')
The draws below stay inside these ranges and needn't reach their ends.
All inputs are finite; a program needn't handle non-finite values. No bound on the sum of `land_sea` on one device may be relied on, other than what follows from the above.
Results may differ from the reference program's by a relative error of at most 0.000098.
Values sent between devices are 32-bit elements; how exact they have to be, the bound alone decides.
A program may use at most 128 MiB of HBM per device.

```python
import jax
import jax.numpy as jnp
from jax import lax

LEV = 144
LAT = 640
PASSES = 10
NSCALE = 8
LON = 512


def draw_roughness(key, part):
    key = jax.random.fold_in(key, 11)
    unit = jax.random.uniform(key, (LEV, LON, LAT), jnp.float32)
    return 0.5 * jnp.exp(unit * jnp.log(2.8))


def draw_scale_table(key, part):
    key = jax.random.fold_in(key, 23)
    unit = jax.random.uniform(key, (NSCALE,), jnp.float32)
    return 0.03 * jnp.exp(unit * jnp.log(4.0))


def set_ends(array, rng, low, high):
    extent = array.shape
    place = [jax.random.randint(jax.random.fold_in(rng, axis), (), 0, extent[axis]) for axis in range(len(extent))]
    array = array.at[tuple(place)].set(low)
    longest = extent.index(max(extent))
    place[longest] = (place[longest] + 1) % extent[longest]
    return array.at[tuple(place)].set(high)


def block_levels(stream_key, shape, pieces, least, top_value):
    def one(axis_at, parts):
        heights = jax.random.uniform(jax.random.fold_in(jax.random.fold_in(stream_key, 6), axis_at), (parts,), jnp.float32, least / len(pieces), top_value / len(pieces))
        return jnp.repeat(jnp.exp(heights), shape[axis_at] // parts).reshape((-1,) + (1,) * (len(shape) - axis_at - 1))

    factor_of = one(*pieces[0])
    for cut in pieces[1:]:
        factor_of = factor_of * one(*cut)
    return factor_of


def normal_values(own_key, extent, deviation, bound, cuts=(), held_as=jnp.bfloat16):
    values = jax.random.normal(own_key, extent, jnp.float32) * deviation
    if len(cuts) > 0:
        values = block_levels(own_key, extent, cuts, -0.22, 0.18) * values
    return jnp.clip(values, min=-bound, max=bound).astype(held_as)


def setup_inputs(seed: int = 0) -> dict:
    streams_of = jax.random.split(jax.random.key(seed), 9)
    gradient = normal_values(streams_of[0], (LEV, 2, LON, LAT), 1.0, 6.0, ((0, 8), (2, 32)), jnp.float32)
    land_sea = set_ends((jax.random.randint(streams_of[1], (LEV, LON, LAT), 0, 16) < 15).astype(jnp.int32), jax.random.fold_in(streams_of[1], 1), 0, 1)
    roughness = draw_roughness(jax.random.fold_in(streams_of[8], 71), 0)
    scale_index = set_ends(jax.random.randint(streams_of[3], (PASSES, LEV), 0, NSCALE), jax.random.fold_in(streams_of[3], 1), 0, NSCALE - 1).astype(jnp.int32)
    scale_table = draw_scale_table(jax.random.fold_in(streams_of[8], 71), 0)
    balance = normal_values(streams_of[5], (LEV, LEV), LEV ** -0.5, 0.5, (), jnp.float32)
    corr_a = normal_values(streams_of[6], (LEV, LEV), LEV ** -0.5, 0.5, (), jnp.float32)
    corr_b = normal_values(streams_of[7], (LEV, LEV), LEV ** -0.5, 0.5, (), jnp.float32)
    return dict(gradient=gradient, land_sea=land_sea, roughness=roughness, scale_index=scale_index, scale_table=scale_table, balance=balance, corr_a=corr_a, corr_b=corr_b)


def lat_spread(weighted):
    upper = jnp.concatenate([weighted[..., 1:], weighted[..., -1:]], -1)
    lower = jnp.concatenate([weighted[..., :1], weighted[..., :-1]], -1)
    return upper + lower - 2.0 * weighted


def reference(gradient, land_sea, roughness, scale_index, scale_table, balance, corr_a, corr_b):
    exact = lax.Precision.HIGHEST
    first_var = gradient[:, 0]
    second_var = gradient[:, 1]
    first = first_var + jnp.einsum("ml,mxy->lxy", balance, second_var, precision=exact)
    out_a = jnp.einsum("lk,lxy->kxy", corr_a, first, precision=exact)
    out_b = jnp.einsum("lk,lxy->kxy", corr_b, second_var, precision=exact)
    field = jnp.stack([out_a, out_b], 1)
    coef = (land_sea.astype(jnp.float32) * roughness)[:, None]
    picks = (scale_index[:, :, None] == jnp.arange(NSCALE, dtype=jnp.int32)[None, None, :]).astype(jnp.float32)
    rates = jnp.sum(picks * scale_table[None, None, :], -1)
    for section in range(PASSES):
        weighted = coef * field
        spread = jnp.roll(weighted, 1, 2) + jnp.roll(weighted, -1, 2) - 2.0 * weighted + lat_spread(weighted)
        field = field + rates[section][:, None, None, None] * coef * spread
    return field
```

```python
import jax
import jax.numpy as jnp
from jax import lax
from jax.experimental import pallas as pl
from jax.experimental.pallas import tpu as pltpu
from jax.sharding import PartitionSpec as P

PASSES = 10
NSCALE = 8
LEVELS = 144
OWN = 18
LON = 16
LAT = 640
LANES = 128
COLS = LAT // LANES
HALO = 10
ROWS = LON + 2 * HALO
MESH = pl.DeviceIdType.MESH
PEERS = ((1, 2), (1, 1), (1, 3), (1, 0), (0, 2), (0, 1), (0, 3))
CHUNKS = ((0, 0), (0, 1), (1, 0), (1, 1))
F32 = jnp.float32
BF16 = jnp.bfloat16


def one_hot(column, shape):
    return (lax.broadcasted_iota(jnp.int32, shape, 1) == column).astype(F32)


def rest_column(row, side):
    owner, pair, level, var = row >> 3, (row >> 2) & 1, (row >> 1) & 1, row & 1
    column = var * 256 + OWN * owner + 16 + level
    return jnp.where(pair == side, column, -1)


def out_rows(side):
    shape = (320, 512)
    row = lax.broadcasted_iota(jnp.int32, shape, 0)
    block, var, owner, level = row >> 7, (row >> 6) & 1, (row >> 3) & 7, row & 7
    main = var * 256 + OWN * owner + 8 * block + level
    return one_hot(jnp.where(row < 256, main, rest_column(row - 256, side)), shape)


def in_rows(side):
    shape = (448, 512)
    row = lax.broadcasted_iota(jnp.int32, shape, 0)
    owner, var, level = row >> 5, (row >> 4) & 1, row & 15
    main = var * 256 + OWN * owner + level
    return one_hot(jnp.where(row < 256, main, rest_column((row - 256) & 63, side)), shape)


def exact_nt(a, b):
    return lax.dot_general(
        a, b, (((1,), (1,)), ((), ())), precision=lax.Precision.HIGHEST, preferred_element_type=F32
    )


def split(x):
    high = x.astype(BF16)
    return high, (x - high.astype(F32)).astype(BF16)


def diffuse(fields, coef, rates):
    lane = lax.broadcasted_iota(jnp.int32, (8, LANES), 1)
    first, last = lane == 0, lane == LANES - 1

    def row_of(ref, row):
        return [ref[row, :, j * LANES : (j + 1) * LANES] for j in range(COLS)]

    def weighted(field, row):
        return [c * f for c, f in zip(row_of(coef, row), row_of(field, row))]

    def one_pass(step, _):
        rate = rates[step]

        def update(row, carry):
            scaled = [rate * c for c in row_of(coef, row)]
            ahead = row_of(coef, row + 1)
            result = []
            for field, (before, now) in zip(fields, carry):
                after = [c * f for c, f in zip(ahead, row_of(field, row + 1))]
                up = [pltpu.roll(w, 1, 1) for w in now]
                down = [pltpu.roll(w, LANES - 1, 1) for w in now]
                for j in range(COLS):
                    lower = jnp.where(first, up[j - 1] if j else now[0], up[j])
                    upper = jnp.where(last, down[j + 1] if j < COLS - 1 else now[j], down[j])
                    spread = (before[j] + after[j]) + (lower + upper) - 4.0 * now[j]
                    own = field[row, :, j * LANES : (j + 1) * LANES]
                    field[row, :, j * LANES : (j + 1) * LANES] = own + scaled[j] * spread
                result.append((now, after))
            return result

        def two(k, carry):
            row = step + 1 + 2 * k
            return update(row + 1, update(row, carry))

        start = [(weighted(f, step), weighted(f, step + 1)) for f in fields]
        lax.fori_loop(0, ROWS // 2 - 1 - step, two, start)
        return 0

    lax.fori_loop(0, PASSES, one_pass, 0)


def kernel(
    grad_hbm, sea_hbm, rough_hbm, index_hbm, table_hbm, balance_hbm, corr_a_hbm, corr_b_hbm, out_hbm,
    grad, sea, rough, index, table, balance, corr_a, corr_b,
    send, send_rest, got, got_rest, mix, mix_rest, field, pairs, rest,
    coef, coef_pairs, coef_rest, rates, natural, weights, operand, result,
    load_sem, small_sem, own_sem, store_sem,
    go_send, go_recv, back_send, back_recv, edge_send, edge_recv, coef_send, coef_recv,
):
    tile, me = lax.axis_index("tile"), lax.axis_index("lev")
    half, y = me // 4, me % 4
    peers = [((half + dx) % 2) * 4 + (y + dy) % 4 for dx, dy in PEERS]
    right, left = (tile + 1) % 32, (tile + 31) % 32

    loads = []
    for n, (source, target) in enumerate(((grad_hbm, grad), (sea_hbm, sea), (rough_hbm, rough))):
        for j in range(COLS):
            copy = pltpu.make_async_copy(
                source.at[:, pl.ds(j * LANES, LANES)], target.at[j], load_sem.at[n, j]
            )
            copy.start()
            loads.append(copy)
    small = []
    pairs_in = (
        (index_hbm, index), (table_hbm, table), (balance_hbm, balance),
        (corr_a_hbm, corr_a), (corr_b_hbm, corr_b),
    )
    for n, (source, target) in enumerate(pairs_in):
        copy = pltpu.make_async_copy(source, target, small_sem.at[n])
        copy.start()
        small.append(copy)

    barrier = pltpu.get_barrier_semaphore()
    for q in peers:
        pl.semaphore_signal(barrier, inc=1, device_id={"lev": q}, device_id_type=MESH)
    for t in (left, right):
        pl.semaphore_signal(barrier, inc=1, device_id={"tile": t}, device_id_type=MESH)

    for copy in loads[:COLS]:
        copy.wait()

    def gather(q, _):
        for i in range(2):
            lon = 2 * q + i
            for j in range(COLS):
                lanes = pl.ds(j * LANES, LANES)
                for v in range(2):
                    for t in range(2):
                        send[q, i, pl.ds(v * 16 + t * 8, 8), lanes] = grad[
                            j, pl.ds(256 * t + 16 * v + lon, 8, stride=32), :
                        ]
                send_rest[q, pl.ds(4 * i, 4), lanes] = grad[j, pl.ds(512 + lon, 4, stride=16), :]
        return 0

    lax.fori_loop(0, 8, gather, 0)
    pl.semaphore_wait(barrier, len(PEERS) + 2)

    def to(q, source, target, sems, at):
        return pltpu.make_async_remote_copy(
            source, target, sems[0].at[at], sems[1].at[at], device_id={"lev": q}, device_id_type=MESH
        )

    go = [[], [], []]
    for part in (2, 0, 1):
        for k, q in enumerate(peers):
            if part < 2:
                copy = to(q, send.at[q, part], got.at[part, me], (go_send, go_recv), (part, k))
            else:
                copy = to(q, send_rest.at[q], got_rest.at[me], (go_send, go_recv), (part, k))
            copy.start()
            go[part].append(copy)
    own = [
        pltpu.make_async_copy(send.at[me, 0], got.at[0, me], own_sem.at[0]),
        pltpu.make_async_copy(send.at[me, 1], got.at[1, me], own_sem.at[1]),
        pltpu.make_async_copy(send_rest.at[me], got_rest.at[me], own_sem.at[2]),
    ]
    for copy in own:
        copy.start()

    for copy in loads[COLS:]:
        copy.wait()

    def coefficients(pair, _):
        for i in range(2):
            lon = 2 * pair + i
            for j in range(COLS):
                lanes = pl.ds(j * LANES, LANES)
                for t in range(2):
                    rows = pl.ds(128 * t + lon, 8, stride=16)
                    coef[t, HALO + lon, :, lanes] = sea[j, rows, :].astype(F32) * rough[j, rows, :]
                for level in range(2):
                    rows = pl.ds(256 + 16 * level + lon, 1)
                    value = sea[j, rows, :].astype(F32) * rough[j, rows, :]
                    coef_pairs[HALO // 2 + pair, pl.ds(4 * i + 2 * level, 2), lanes] = jnp.broadcast_to(
                        value, (2, LANES)
                    )
        return 0

    lax.fori_loop(0, 8, coefficients, 0)

    def edges(ref, span, width, sems, at):
        copies = []
        for n, (target, source, landing) in enumerate(
            ((right, span, 0), (left, width, width + span))
        ):
            copy = pltpu.make_async_remote_copy(
                ref.at[pl.ds(source, width)], ref.at[pl.ds(landing, width)],
                sems[0].at[at, n], sems[1].at[at, n],
                device_id={"tile": target}, device_id_type=MESH,
            )
            copy.start()
            copies.append(copy)
        return copies

    coef_sems = (coef_send, coef_recv)
    coef_edges = [edges(coef.at[t], LON, HALO, coef_sems, t) for t in range(2)]
    coef_edges.append(edges(coef_pairs, LON // 2, HALO // 2, coef_sems, 2))

    for copy in small:
        copy.wait()
    picked = jnp.zeros((PASSES, LEVELS), F32)
    for n in range(NSCALE):
        picked = jnp.where(index[...] == n, table[n], picked)
    column = lax.broadcasted_iota(jnp.int32, (8, LEVELS), 1) - OWN * me
    row = lax.broadcasted_iota(jnp.int32, (8, LEVELS), 0)
    for t, level in enumerate((row, row + 8, 16 + ((row >> 1) & 1))):
        for p in range(PASSES):
            chosen = jnp.where(column == level, jnp.broadcast_to(picked[p : p + 1], (8, LEVELS)), 0.0)
            rates[t, p] = jnp.broadcast_to(jnp.sum(chosen, axis=1, keepdims=True), (8, LANES))

    natural[...] = jnp.zeros((512, 512), F32)
    natural[0:LEVELS, 0:LEVELS] = corr_a[...]
    natural[256 : 256 + LEVELS, 0:LEVELS] = jnp.dot(
        balance[...], corr_a[...], precision=lax.Precision.HIGHEST, preferred_element_type=F32
    )
    natural[256 : 256 + LEVELS, 256 : 256 + LEVELS] = corr_b[...]
    for i in range(2):
        half_way = exact_nt(out_rows(i), natural[...])
        full = exact_nt(half_way, in_rows(i))
        high, low = split(full[:, :256])
        weights[i, :, 0:256] = high
        weights[i, :, 256:512] = high
        weights[i, :, 512:768] = low
        tail = full[:, 256:]
        high = tail.astype(BF16).astype(F32)
        at = lax.broadcasted_iota(jnp.int32, (320, 192), 1)
        weights[i, :, 768:960] = jnp.where(at < 128, high, tail - high).astype(BF16)

    def take(i):
        def block(p, _):
            high, low = split(got[i, p])
            rows = pl.multiple_of(p * 32, 32)
            operand[i, pl.ds(rows, 32), :] = high
            operand[i, pl.ds(256 + rows, 32), :] = low
            operand[i, pl.ds(512 + rows, 32), :] = high
            return 0

        lax.fori_loop(0, 8, block, 0)

    own[2].wait()
    for copy in go[2]:
        copy.wait_recv()
    high, low = split(got_rest[...].reshape(64, LAT))
    for i in range(2):
        operand[i, 768:832, :] = high
        operand[i, 832:896, :] = low
        operand[i, 896:960, :] = high
    for i in range(2):
        own[i].wait()
        for copy in go[i]:
            copy.wait_recv()
        take(i)

    back = []
    for t in range(2):
        for i in range(2):
            mixed = jnp.dot(
                weights[i, 128 * t : 128 * (t + 1), :], operand[i], preferred_element_type=F32
            )
            mix[t, :, :, i] = mixed.reshape(2, 8, 8, LAT)
        for v in range(2):
            copies = []
            rows = pl.ds(HALO + 2 * me, 2)
            for k, q in enumerate(peers):
                copy = to(q, mix.at[t, v, q], field.at[t, v, rows], (back_send, back_recv), (2 * t + v, k))
                copy.start()
                copies.append(copy)
            copy = pltpu.make_async_copy(mix.at[t, v, me], field.at[t, v, rows], own_sem.at[3 + 2 * t + v])
            copy.start()
            back.append((copies, copy))
    mixed = jnp.dot(weights[0, 256:320, :], operand[0], preferred_element_type=F32)
    mixed = mixed + jnp.dot(weights[1, 256:320, :], operand[1], preferred_element_type=F32)
    mix_rest[...] = mixed.reshape(8, 8, LAT)
    copies = []
    for k, q in enumerate(peers):
        copy = to(q, mix_rest.at[q], pairs.at[HALO // 2 + me], (back_send, back_recv), (4, k))
        copy.start()
        copies.append(copy)
    copy = pltpu.make_async_copy(mix_rest.at[me], pairs.at[HALO // 2 + me], own_sem.at[7])
    copy.start()
    back.append((copies, copy))

    edge_sems = (edge_send, edge_recv)

    def arrive(n):
        copies, local = back[n]
        local.wait()
        for copy in copies:
            copy.wait_recv()
        if n < 4:
            return edges(field.at[n // 2, n % 2], LON, HALO, edge_sems, n)
        return edges(pairs, LON // 2, HALO // 2, edge_sems, n)

    def settle(copies):
        for copy in copies:
            copy.wait()

    stores = []

    def store(rows, count, at):
        for j in range(COLS):
            copy = pltpu.make_async_copy(
                result.at[j, pl.ds(rows, count)],
                out_hbm.at[pl.ds(rows, count), pl.ds(j * LANES, LANES)],
                store_sem.at[at, j],
            )
            copy.start()
            stores.append(copy)

    def finish(t, v):
        def place(lon, _):
            for j in range(COLS):
                result[j, pl.ds(256 * t + 16 * v + lon, 8, stride=32), :] = field[
                    t, v, HALO + lon, :, j * LANES : (j + 1) * LANES
                ]
            return 0

        lax.fori_loop(0, LON, place, 0)

    def unpack(source, target, masked):
        top = lax.broadcasted_iota(jnp.int32, (8, LANES), 0) < 4

        def one(pair, _):
            for j in range(COLS):
                lanes = slice(j * LANES, (j + 1) * LANES)
                value = source[pair, :, lanes]
                turned = pltpu.roll(value, 4, 0)
                if masked:
                    value, turned = jnp.where(top, value, 0.0), jnp.where(top, turned, 0.0)
                target[2 * pair, :, lanes] = value
                target[2 * pair + 1, :, lanes] = turned
            return 0

        lax.fori_loop(0, ROWS // 2, one, 0)

    moving = [arrive(0), arrive(1)]
    settle(coef_edges[0])
    settle(coef_edges[1])
    settle(coef_edges[2])
    unpack(coef_pairs, coef_rest, True)
    settle(moving[0])
    settle(moving[1])
    diffuse([field.at[0, 0], field.at[0, 1]], coef.at[0], rates.at[0])
    moving.append(arrive(2))
    moving.append(arrive(3))
    moving.append(arrive(4))
    finish(0, 0)
    finish(0, 1)
    store(0, 256, 0)
    settle(moving[2])
    settle(moving[3])
    diffuse([field.at[1, 0], field.at[1, 1]], coef.at[1], rates.at[1])
    finish(1, 0)
    finish(1, 1)
    store(256, 256, 1)
    settle(moving[4])
    unpack(pairs, rest, False)
    diffuse([rest], coef_rest, rates.at[2])

    def place_rest(lon, _):
        for j in range(COLS):
            result[j, pl.ds(512 + lon, 4, stride=16), :] = rest[
                HALO + lon, 0:4, j * LANES : (j + 1) * LANES
            ]
        return 0

    lax.fori_loop(0, LON, place_rest, 0)
    store(512, 64, 2)
    for copies in go:
        for copy in copies:
            copy.wait_send()
    for copies, _ in back:
        for copy in copies:
            copy.wait_send()
    for copy in stores:
        copy.wait()


def on_device(gradient, land_sea, roughness, scale_index, scale_table, balance, corr_a, corr_b):
    hbm = pl.BlockSpec(memory_space=pl.ANY)
    vmem, dma = pltpu.VMEM, pltpu.SemaphoreType.DMA
    out = pl.pallas_call(
        kernel,
        out_shape=jax.ShapeDtypeStruct((OWN * 2 * LON, LAT), F32),
        in_specs=[hbm] * 8,
        out_specs=hbm,
        scratch_shapes=[
            vmem((COLS, OWN * 2 * LON, LANES), F32),
            vmem((COLS, OWN * LON, LANES), jnp.int32),
            vmem((COLS, OWN * LON, LANES), F32),
            vmem((PASSES, LEVELS), jnp.int32),
            pltpu.SMEM((NSCALE,), F32),
            vmem((LEVELS, LEVELS), F32),
            vmem((LEVELS, LEVELS), F32),
            vmem((LEVELS, LEVELS), F32),
            vmem((8, 2, 32, LAT), F32),
            vmem((8, 8, LAT), F32),
            vmem((2, 8, 32, LAT), F32),
            vmem((8, 8, LAT), F32),
            vmem((2, 2, 8, 2, 8, LAT), F32),
            vmem((8, 8, LAT), F32),
            vmem((2, 2, ROWS, 8, LAT), F32),
            vmem((ROWS // 2, 8, LAT), F32),
            vmem((ROWS, 8, LAT), F32),
            vmem((2, ROWS, 8, LAT), F32),
            vmem((ROWS // 2, 8, LAT), F32),
            vmem((ROWS, 8, LAT), F32),
            vmem((3, PASSES, 8, LANES), F32),
            vmem((512, 512), F32),
            vmem((2, 320, 960), BF16),
            vmem((2, 960, LAT), BF16),
            vmem((COLS, OWN * 2 * LON, LANES), F32),
            dma((3, COLS)),
            dma((5,)),
            dma((8,)),
            dma((3, COLS)),
            dma((3, 7)),
            dma((3, 7)),
            dma((5, 7)),
            dma((5, 7)),
            dma((5, 2)),
            dma((5, 2)),
            dma((3, 2)),
            dma((3, 2)),
        ],
        compiler_params=pltpu.CompilerParams(
            collective_id=0, has_side_effects=True, vmem_limit_bytes=56 * 2**20
        ),
    )(
        gradient.reshape(OWN * 2 * LON, LAT),
        land_sea.reshape(OWN * LON, LAT),
        roughness.reshape(OWN * LON, LAT),
        scale_index,
        scale_table,
        balance,
        corr_a,
        corr_b,
    )
    return out.reshape(OWN, 2, LON, LAT)


def solution(mesh):
    return jax.shard_map(
        on_device,
        mesh=mesh,
        in_specs=(
            P("lev", None, "tile", None),
            P("lev", "tile", None),
            P("lev", "tile", None),
            P(),
            P(),
            P(),
            P(),
            P(),
        ),
        out_specs=P("lev", None, "tile", None),
        check_vma=False,
    )
```

```python
import jax
import jax.numpy as jnp
from jax import lax
from jax.experimental import pallas as pl
from jax.experimental.pallas import tpu as pltpu
from jax.sharding import PartitionSpec as P

PASSES = 10
NSCALE = 8
LEVELS = 144
OWN = 18
LON = 16
LAT = 640
LANES = 128
COLS = LAT // LANES
HALO = 10
ROWS = LON + 2 * HALO
MESH = pl.DeviceIdType.MESH
PEERS = ((1, 2), (1, 1), (1, 3), (1, 0), (0, 2), (0, 1), (0, 3))
F32 = jnp.float32
BF16 = jnp.bfloat16


def one_hot(column, shape):
    return (lax.broadcasted_iota(jnp.int32, shape, 1) == column).astype(F32)


def rest_column(row, side):
    owner, pair, level, var = row >> 3, (row >> 2) & 1, (row >> 1) & 1, row & 1
    column = var * 256 + OWN * owner + 16 + level
    return jnp.where(pair == side, column, -1)


def out_rows(side):
    shape = (320, 512)
    row = lax.broadcasted_iota(jnp.int32, shape, 0)
    block, var, owner, level = row >> 7, (row >> 6) & 1, (row >> 3) & 7, row & 7
    main = var * 256 + OWN * owner + 8 * block + level
    return one_hot(jnp.where(row < 256, main, rest_column(row - 256, side)), shape)


def in_rows(side):
    shape = (448, 512)
    row = lax.broadcasted_iota(jnp.int32, shape, 0)
    owner, var, level = row >> 5, (row >> 4) & 1, row & 15
    main = var * 256 + OWN * owner + level
    return one_hot(jnp.where(row < 256, main, rest_column((row - 256) & 63, side)), shape)


def exact_nt(a, b):
    return lax.dot_general(
        a, b, (((1,), (1,)), ((), ())), precision=lax.Precision.HIGHEST, preferred_element_type=F32
    )


def split(x):
    high = x.astype(BF16)
    return high, (x - high.astype(F32)).astype(BF16)


def permuted(x, order):
    high = x.astype(BF16)
    middle, low = split(x - high.astype(F32))
    return (moved(high, order) + moved(middle, order)) + moved(low, order)


def moved(x, order):
    return jnp.dot(x, order, preferred_element_type=F32)


def diffuse(field, coef, rates):
    lane = lax.broadcasted_iota(jnp.int32, (8, LANES), 1)
    first, last = lane == 0, lane == LANES - 1
    ahead = 3

    def row_of(ref, row):
        return [ref[row, :, j * LANES : (j + 1) * LANES] for j in range(COLS)]

    def ends(w):
        return (
            jnp.where(first, w[0], pltpu.roll(w[-1], 1, 1)),
            jnp.where(last, w[-1], pltpu.roll(w[0], LANES - 1, 1)),
        )

    for step in range(PASSES):
        rate = rates[step]
        low, high = step + 1, ROWS - 1 - step
        rows, outer = {low - 1: row_of(field, low - 1)}, {}
        for row in range(low, low + ahead):
            rows[row] = row_of(field, row)
            outer[row] = ends(rows[row])
        for row in range(low, high):
            if row + ahead <= high:
                rows[row + ahead] = row_of(field, row + ahead)
                outer[row + ahead] = ends(rows[row + ahead])
            before, now, after = rows[row - 1], rows[row], rows[row + 1]
            line = [outer[row][0]] + now + [outer[row][1]]
            for j, c in enumerate(row_of(coef, row)):
                total = (before[j] + after[j]) + (line[j] + line[j + 2])
                field[row, :, j * LANES : (j + 1) * LANES] = now[j] + (rate * c) * (total - 4.0 * now[j])


def unpack(source, target):
    top = lax.broadcasted_iota(jnp.int32, (8, LANES), 0) < 4

    def one(pair, _):
        for j in range(COLS):
            lanes = slice(j * LANES, (j + 1) * LANES)
            value = source[pair, :, lanes]
            target[2 * pair, :, lanes] = jnp.where(top, value, 0.0)
            target[2 * pair + 1, :, lanes] = jnp.where(top, pltpu.roll(value, 4, 0), 0.0)
        return 0

    lax.fori_loop(0, ROWS // 2, one, 0)


def kernel(
    grad_hbm, sea_hbm, rough_hbm, index_hbm, table_hbm, balance_hbm, corr_a_hbm, corr_b_hbm, out_hbm,
    grad, sea, rough, index, table, balance, corr_a, corr_b,
    send, send_rest, got, got_rest, mix, mix_rest, land, land_rest, wave, wave_pairs,
    coef, coef_pairs, square, square_pairs, rates, natural, weights, operand, order, back_order, result,
    load_sem, small_sem, own_sem, store_sem,
    go_send, go_recv, back_send, back_recv, edge_send, edge_recv, coef_send, coef_recv,
):
    tile, me = lax.axis_index("tile"), lax.axis_index("lev")
    half, y = me // 4, me % 4
    peers = [((half + dx) % 2) * 4 + (y + dy) % 4 for dx, dy in PEERS]
    right, left = (tile + 1) % 32, (tile + 31) % 32

    loads = []
    for n, (source, target) in enumerate(((grad_hbm, grad), (sea_hbm, sea), (rough_hbm, rough))):
        for j in range(COLS):
            copy = pltpu.make_async_copy(
                source.at[:, pl.ds(j * LANES, LANES)], target.at[j], load_sem.at[n, j]
            )
            copy.start()
            loads.append(copy)
    small = []
    pairs_in = (
        (index_hbm, index), (table_hbm, table), (balance_hbm, balance),
        (corr_a_hbm, corr_a), (corr_b_hbm, corr_b),
    )
    for n, (source, target) in enumerate(pairs_in):
        copy = pltpu.make_async_copy(source, target, small_sem.at[n])
        copy.start()
        small.append(copy)

    barrier = pltpu.get_barrier_semaphore()
    for q in peers:
        pl.semaphore_signal(barrier, inc=1, device_id={"lev": q}, device_id_type=MESH)
    for t in (left, right):
        pl.semaphore_signal(barrier, inc=1, device_id={"tile": t}, device_id_type=MESH)

    for copy in loads[:COLS]:
        copy.wait()

    def gather(q, _):
        for i in range(2):
            lon = 2 * q + i
            for j in range(COLS):
                lanes = pl.ds(j * LANES, LANES)
                for v in range(2):
                    for t in range(2):
                        send[q, i, pl.ds(v * 16 + t * 8, 8), lanes] = grad[
                            j, pl.ds(256 * t + 16 * v + lon, 8, stride=32), :
                        ]
                send_rest[q, pl.ds(4 * i, 4), lanes] = grad[j, pl.ds(512 + lon, 4, stride=16), :]
        return 0

    lax.fori_loop(0, 8, gather, 0)
    pl.semaphore_wait(barrier, len(PEERS) + 2)

    def to(q, source, target, sems, at):
        return pltpu.make_async_remote_copy(
            source, target, sems[0].at[at], sems[1].at[at], device_id={"lev": q}, device_id_type=MESH
        )

    go = [[], [], []]
    for part in (2, 0, 1):
        for k, q in enumerate(peers):
            if part < 2:
                copy = to(q, send.at[q, part], got.at[part, me], (go_send, go_recv), (part, k))
            else:
                copy = to(q, send_rest.at[q], got_rest.at[me], (go_send, go_recv), (part, k))
            copy.start()
            go[part].append(copy)
    own = [
        pltpu.make_async_copy(send.at[me, 0], got.at[0, me], own_sem.at[0]),
        pltpu.make_async_copy(send.at[me, 1], got.at[1, me], own_sem.at[1]),
        pltpu.make_async_copy(send_rest.at[me], got_rest.at[me], own_sem.at[2]),
    ]
    for copy in own:
        copy.start()

    row = lax.broadcasted_iota(jnp.int32, (LAT, LAT), 0)
    column = lax.broadcasted_iota(jnp.int32, (LAT, LAT), 1)
    order[...] = (row == COLS * (column & 127) + (column >> 7)).astype(F32).astype(BF16)
    back_order[...] = (column == COLS * (row & 127) + (row >> 7)).astype(F32).astype(BF16)

    for copy in loads[COLS:]:
        copy.wait()

    def coefficients(pair, _):
        for i in range(2):
            lon = 2 * pair + i
            for j in range(COLS):
                lanes = pl.ds(j * LANES, LANES)
                for t in range(2):
                    rows = pl.ds(128 * t + lon, 8, stride=16)
                    coef[t, lon, :, lanes] = sea[j, rows, :].astype(F32) * rough[j, rows, :]
                for level in range(2):
                    rows = pl.ds(256 + 16 * level + lon, 1)
                    value = sea[j, rows, :].astype(F32) * rough[j, rows, :]
                    coef_pairs[pair, pl.ds(4 * i + 2 * level, 2), lanes] = jnp.broadcast_to(
                        value, (2, LANES)
                    )
        return 0

    lax.fori_loop(0, 8, coefficients, 0)
    for t in range(2):
        value = permuted(coef[t].reshape(LON * 8, LAT), order[...]).reshape(LON, 8, LAT)
        coef[t] = value
        square[t, HALO : HALO + LON] = value * value
    value = permuted(coef_pairs[...].reshape(64, LAT), order[...]).reshape(8, 8, LAT)
    coef_pairs[...] = value
    square_pairs[HALO // 2 : HALO // 2 + 8] = value * value

    def edges(ref, span, width, sems, at):
        copies = []
        for n, (target, source, landing) in enumerate(
            ((right, span, 0), (left, width, width + span))
        ):
            copies.append(
                pltpu.make_async_remote_copy(
                    ref.at[pl.ds(source, width)], ref.at[pl.ds(landing, width)],
                    sems[0].at[at, n], sems[1].at[at, n],
                    device_id={"tile": target}, device_id_type=MESH,
                )
            )
        return copies

    coef_sems = (coef_send, coef_recv)
    coef_edges = [edges(square.at[t], LON, HALO, coef_sems, t) for t in range(2)]
    coef_edges.append(edges(square_pairs, LON // 2, HALO // 2, coef_sems, 2))
    for copies in coef_edges:
        for copy in copies:
            copy.start()

    for copy in small:
        copy.wait()
    picked = jnp.zeros((PASSES, LEVELS), F32)
    for n in range(NSCALE):
        picked = jnp.where(index[...] == n, table[n], picked)
    column = lax.broadcasted_iota(jnp.int32, (8, LEVELS), 1) - OWN * me
    row = lax.broadcasted_iota(jnp.int32, (8, LEVELS), 0)
    for t, level in enumerate((row, row + 8, 16 + ((row >> 1) & 1))):
        for p in range(PASSES):
            chosen = jnp.where(column == level, jnp.broadcast_to(picked[p : p + 1], (8, LEVELS)), 0.0)
            rates[t, p] = jnp.broadcast_to(jnp.sum(chosen, axis=1, keepdims=True), (8, LANES))

    natural[...] = jnp.zeros((512, 512), F32)
    natural[0:LEVELS, 0:LEVELS] = corr_a[...]
    natural[256 : 256 + LEVELS, 0:LEVELS] = jnp.dot(
        balance[...], corr_a[...], precision=lax.Precision.HIGHEST, preferred_element_type=F32
    )
    natural[256 : 256 + LEVELS, 256 : 256 + LEVELS] = corr_b[...]
    for i in range(2):
        half_way = exact_nt(out_rows(i), natural[...])
        full = exact_nt(half_way, in_rows(i))
        high, low = split(full[:, :256])
        weights[i, :, 0:256] = high
        weights[i, :, 256:512] = high
        weights[i, :, 512:768] = low
        tail = full[:, 256:]
        high = tail.astype(BF16).astype(F32)
        at = lax.broadcasted_iota(jnp.int32, (320, 192), 1)
        weights[i, :, 768:960] = jnp.where(at < 128, high, tail - high).astype(BF16)

    def take(x, places):
        high, low = split(x)
        high, low = moved(high, order[...]).astype(BF16), moved(low, order[...]).astype(BF16)
        count = x.shape[0]
        for i, start in places:
            operand[i, start : start + count, :] = high
            operand[i, start + count : start + 2 * count, :] = low
            operand[i, start + 2 * count : start + 3 * count, :] = high

    own[2].wait()
    for copy in go[2]:
        copy.wait_recv()
    take(got_rest[...].reshape(64, LAT), ((0, 768), (1, 768)))
    for i in range(2):
        own[i].wait()
        for copy in go[i]:
            copy.wait_recv()
        take(got[i].reshape(256, LAT), ((i, 0),))

    back_sems = (back_send, back_recv)

    def back(n):
        if n < 4:
            source, target = mix.at[n], land.at[n, pl.ds(2 * me, 2)]
        else:
            source, target = mix_rest, land_rest.at[me]
        remote = [to(q, source.at[q], target, back_sems, (n, k)) for k, q in enumerate(peers)]
        return remote, pltpu.make_async_copy(source.at[me], target, own_sem.at[3 + n])

    def start_back(n):
        remote, local = back(n)
        for copy in remote:
            copy.start()
        local.start()

    for t in range(2):
        for i in range(2):
            mixed = jnp.dot(
                weights[i, 128 * t : 128 * (t + 1), :], operand[i], preferred_element_type=F32
            )
            mix[2 * t : 2 * t + 2, :, i] = mixed.reshape(2, 8, 8, LAT)
        start_back(2 * t)
        start_back(2 * t + 1)
    mixed = jnp.dot(weights[0, 256:320, :], operand[0], preferred_element_type=F32)
    mixed = mixed + jnp.dot(weights[1, 256:320, :], operand[1], preferred_element_type=F32)
    mix_rest[...] = mixed.reshape(8, 8, LAT)
    start_back(4)

    edge_sems = (edge_send, edge_recv)

    def sides(n):
        if n < 4:
            return edges(wave.at[n], LON, HALO, edge_sems, n)
        return edges(wave_pairs, LON // 2, HALO // 2, edge_sems, n)

    def arrive(n):
        remote, local = back(n)
        local.wait()
        for copy in remote:
            copy.wait_recv()
        if n < 4:
            wave[n, HALO : HALO + LON] = land[n] * coef[n // 2]
        else:
            wave_pairs[HALO // 2 : HALO // 2 + 8] = land_rest[...] * coef_pairs[...]
        for copy in sides(n):
            copy.start()

    def store(rows, count, at):
        return [
            pltpu.make_async_copy(
                result.at[j, pl.ds(rows, count)],
                out_hbm.at[pl.ds(rows, count), pl.ds(j * LANES, LANES)],
                store_sem.at[at, j],
            )
            for j in range(COLS)
        ]

    def unweighted(value, c, mixed, count):
        value = jnp.where(c == 0.0, mixed, value / jnp.where(c == 0.0, 1.0, c)).reshape(count, LAT)
        high, low = split(value)
        return moved(high, back_order[...]) + moved(low, back_order[...])

    arrive(0)
    for copies in coef_edges:
        for copy in copies:
            copy.wait()
    unpack(square_pairs, square.at[2])

    def plane(n, _):
        for k in range(5):

            @pl.when(n == k)
            def _():
                if k < 4:
                    arrive(k + 1)
                for copy in sides(k):
                    copy.wait()
                if k == 4:
                    unpack(wave_pairs, wave.at[4])

        diffuse(wave.at[n], square.at[n // 2], rates.at[n // 2])

        @pl.when(n < 4)
        def _():
            t, v = n // 2, n % 2
            value = unweighted(wave[n, HALO : HALO + LON], coef[t], land[n], LON * 8)
            for lon in range(LON):
                for j in range(COLS):
                    result[j, pl.ds(256 * t + 16 * v + lon, 8, stride=32), :] = value[
                        8 * lon : 8 * lon + 8, j * LANES : (j + 1) * LANES
                    ]

        for t in range(2):

            @pl.when(n == 2 * t + 1)
            def _():
                for copy in store(256 * t, 256, t):
                    copy.start()

        return 0

    lax.fori_loop(0, 5, plane, 0)

    top = lax.broadcasted_iota(jnp.int32, (8, LAT), 0) < 4
    packed = [
        jnp.where(top, wave[4, HALO + 2 * p], pltpu.roll(wave[4, HALO + 2 * p + 1], 4, 0))[None]
        for p in range(8)
    ]
    value = unweighted(jnp.concatenate(packed, 0), coef_pairs[...], land_rest[...], 64)
    for lon in range(LON):
        for j in range(COLS):
            result[j, pl.ds(512 + lon, 4, stride=16), :] = value[
                4 * lon : 4 * lon + 4, j * LANES : (j + 1) * LANES
            ]
    for copy in store(512, 64, 2):
        copy.start()
    for copies in go:
        for copy in copies:
            copy.wait_send()
    for n in range(5):
        for copy in back(n)[0]:
            copy.wait_send()
    for at, (rows, count) in enumerate(((0, 256), (256, 256), (512, 64))):
        for copy in store(rows, count, at):
            copy.wait()


def on_device(gradient, land_sea, roughness, scale_index, scale_table, balance, corr_a, corr_b):
    hbm = pl.BlockSpec(memory_space=pl.ANY)
    vmem, dma = pltpu.VMEM, pltpu.SemaphoreType.DMA
    out = pl.pallas_call(
        kernel,
        out_shape=jax.ShapeDtypeStruct((OWN * 2 * LON, LAT), F32),
        in_specs=[hbm] * 8,
        out_specs=hbm,
        scratch_shapes=[
            vmem((COLS, OWN * 2 * LON, LANES), F32),
            vmem((COLS, OWN * LON, LANES), jnp.int32),
            vmem((COLS, OWN * LON, LANES), F32),
            vmem((PASSES, LEVELS), jnp.int32),
            pltpu.SMEM((NSCALE,), F32),
            vmem((LEVELS, LEVELS), F32),
            vmem((LEVELS, LEVELS), F32),
            vmem((LEVELS, LEVELS), F32),
            vmem((8, 2, 32, LAT), F32),
            vmem((8, 8, LAT), F32),
            vmem((2, 8, 32, LAT), F32),
            vmem((8, 8, LAT), F32),
            vmem((4, 8, 2, 8, LAT), F32),
            vmem((8, 8, LAT), F32),
            vmem((4, LON, 8, LAT), F32),
            vmem((8, 8, LAT), F32),
            vmem((5, ROWS, 8, LAT), F32),
            vmem((ROWS // 2, 8, LAT), F32),
            vmem((2, LON, 8, LAT), F32),
            vmem((8, 8, LAT), F32),
            vmem((3, ROWS, 8, LAT), F32),
            vmem((ROWS // 2, 8, LAT), F32),
            vmem((3, PASSES, 8, LANES), F32),
            vmem((512, 512), F32),
            vmem((2, 320, 960), BF16),
            vmem((2, 960, LAT), BF16),
            vmem((LAT, LAT), BF16),
            vmem((LAT, LAT), BF16),
            vmem((COLS, OWN * 2 * LON, LANES), F32),
            dma((3, COLS)),
            dma((5,)),
            dma((8,)),
            dma((3, COLS)),
            dma((3, 7)),
            dma((3, 7)),
            dma((5, 7)),
            dma((5, 7)),
            dma((5, 2)),
            dma((5, 2)),
            dma((3, 2)),
            dma((3, 2)),
        ],
        compiler_params=pltpu.CompilerParams(
            collective_id=0, has_side_effects=True, vmem_limit_bytes=56 * 2**20
        ),
    )(
        gradient.reshape(OWN * 2 * LON, LAT),
        land_sea.reshape(OWN * LON, LAT),
        roughness.reshape(OWN * LON, LAT),
        scale_index,
        scale_table,
        balance,
        corr_a,
        corr_b,
    )
    return out.reshape(OWN, 2, LON, LAT)


def solution(mesh):
    return jax.shard_map(
        on_device,
        mesh=mesh,
        in_specs=(
            P("lev", None, "tile", None),
            P("lev", "tile", None),
            P("lev", "tile", None),
            P(),
            P(),
            P(),
            P(),
            P(),
        ),
        out_specs=P("lev", None, "tile", None),
        check_vma=False,
    )
```

```python
import jax
import jax.numpy as jnp
from jax import lax
from jax.experimental import pallas as pl
from jax.experimental.pallas import tpu as pltpu
from jax.sharding import PartitionSpec as P

PASSES = 10
NSCALE = 8
LEVELS = 144
OWN = 18
LON = 16
LAT = 640
LANES = 128
COLS = LAT // LANES
HALO = 10
ROWS = LON + 2 * HALO
MESH = pl.DeviceIdType.MESH
PEERS = ((1, 2), (1, 1), (1, 3), (1, 0), (0, 2), (0, 1), (0, 3))
STOPS = (1, 2)
FIELD_STOPS = (1, 2, 0, 0, 0)
COEF_STOPS = (1, 2, 0)
F32 = jnp.float32
BF16 = jnp.bfloat16


def one_hot(column, shape):
    return (lax.broadcasted_iota(jnp.int32, shape, 1) == column).astype(F32)


def rest_column(row, side):
    owner, pair, level, var = row >> 3, (row >> 2) & 1, (row >> 1) & 1, row & 1
    column = var * 256 + OWN * owner + 16 + level
    return jnp.where(pair == side, column, -1)


def out_rows(side):
    shape = (320, 512)
    row = lax.broadcasted_iota(jnp.int32, shape, 0)
    block, var, owner, level = row >> 7, (row >> 6) & 1, (row >> 3) & 7, row & 7
    main = var * 256 + OWN * owner + 8 * block + level
    return one_hot(jnp.where(row < 256, main, rest_column(row - 256, side)), shape)


def in_rows(side):
    shape = (448, 512)
    row = lax.broadcasted_iota(jnp.int32, shape, 0)
    owner, var, level = row >> 5, (row >> 4) & 1, row & 15
    main = var * 256 + OWN * owner + level
    return one_hot(jnp.where(row < 256, main, rest_column((row - 256) & 63, side)), shape)


def exact_nt(a, b):
    return lax.dot_general(
        a, b, (((1,), (1,)), ((), ())), precision=lax.Precision.HIGHEST, preferred_element_type=F32
    )


def split(x):
    high = x.astype(BF16)
    return high, (x - high.astype(F32)).astype(BF16)


def permuted(x, order):
    high = x.astype(BF16)
    middle, low = split(x - high.astype(F32))
    return (moved(high, order) + moved(middle, order)) + moved(low, order)


def moved(x, order):
    return jnp.dot(x, order, preferred_element_type=F32)


def diffuse(field, coef, rates):
    lane = lax.broadcasted_iota(jnp.int32, (8, LANES), 1)
    first, last = lane == 0, lane == LANES - 1
    ahead = 3

    def row_of(ref, row):
        return [ref[row, :, j * LANES : (j + 1) * LANES] for j in range(COLS)]

    def ends(w):
        return (
            jnp.where(first, w[0], pltpu.roll(w[-1], 1, 1)),
            jnp.where(last, w[-1], pltpu.roll(w[0], LANES - 1, 1)),
        )

    for step in range(PASSES):
        rate = rates[step]
        low, high = step + 1, ROWS - 1 - step
        rows, outer = {low - 1: row_of(field, low - 1)}, {}
        for row in range(low, low + ahead):
            rows[row] = row_of(field, row)
            outer[row] = ends(rows[row])
        for row in range(low, high):
            if row + ahead <= high:
                rows[row + ahead] = row_of(field, row + ahead)
                outer[row + ahead] = ends(rows[row + ahead])
            before, now, after = rows[row - 1], rows[row], rows[row + 1]
            line = [outer[row][0]] + now + [outer[row][1]]
            for j, c in enumerate(row_of(coef, row)):
                total = (before[j] + after[j]) + (line[j] + line[j + 2])
                field[row, :, j * LANES : (j + 1) * LANES] = now[j] + (rate * c) * (total - 4.0 * now[j])


def unpack(source, target):
    top = lax.broadcasted_iota(jnp.int32, (8, LANES), 0) < 4

    def one(pair, _):
        for j in range(COLS):
            lanes = slice(j * LANES, (j + 1) * LANES)
            value = source[pair, :, lanes]
            target[2 * pair, :, lanes] = jnp.where(top, value, 0.0)
            target[2 * pair + 1, :, lanes] = jnp.where(top, pltpu.roll(value, 4, 0), 0.0)
        return 0

    lax.fori_loop(0, ROWS // 2, one, 0)


def kernel(
    grad_hbm, sea_hbm, rough_hbm, index_hbm, table_hbm, balance_hbm, corr_a_hbm, corr_b_hbm, out_hbm,
    grad, sea, rough, index, table, balance, corr_a, corr_b,
    send, send_rest, got, got_rest, mix, mix_rest, land, land_rest, wave, wave_pairs,
    coef, coef_pairs, square, square_pairs, rates, natural, weights, operand, order, back_order, result,
    stop, stop_coef,
    load_sem, small_sem, own_sem, store_sem,
    go_send, go_recv, back_send, back_recv, edge_send, edge_recv, coef_send, coef_recv, stop_send, stop_recv,
):
    tile, me = lax.axis_index("tile"), lax.axis_index("lev")
    half, y = me // 4, me % 4
    peers = [((half + dx) % 2) * 4 + (y + dy) % 4 for dx, dy in PEERS]
    right, left = (tile + 1) % 32, (tile + 31) % 32

    loads = []
    for n, (source, target) in enumerate(((grad_hbm, grad), (sea_hbm, sea), (rough_hbm, rough))):
        for j in range(COLS):
            copy = pltpu.make_async_copy(
                source.at[:, pl.ds(j * LANES, LANES)], target.at[j], load_sem.at[n, j]
            )
            copy.start()
            loads.append(copy)
    small = []
    pairs_in = (
        (index_hbm, index), (table_hbm, table), (balance_hbm, balance),
        (corr_a_hbm, corr_a), (corr_b_hbm, corr_b),
    )
    for n, (source, target) in enumerate(pairs_in):
        copy = pltpu.make_async_copy(source, target, small_sem.at[n])
        copy.start()
        small.append(copy)

    barrier = pltpu.get_barrier_semaphore()
    for q in peers:
        pl.semaphore_signal(barrier, inc=1, device_id={"lev": q}, device_id_type=MESH)
    for t in (left, right):
        pl.semaphore_signal(barrier, inc=1, device_id={"tile": t}, device_id_type=MESH)

    place = tile % 16

    def around(steps):
        return (tile + steps + 48) % 32

    def stops(d):
        return ((place == 15, place == 15 - 2 * d, 1), (place == 0, place == 2 * d, -1))

    def greet(t):
        pl.semaphore_signal(barrier, inc=1, device_id={"tile": t}, device_id_type=MESH)

    for d in STOPS:
        for at_seam, at_stop, way in stops(d):

            @pl.when(at_stop)
            def _():
                greet(around(2 * d * way))

            @pl.when(at_seam)
            def _():
                greet(around((2 * d + 1) * way))

    for copy in loads[:COLS]:
        copy.wait()

    def gather(q, _):
        for i in range(2):
            lon = 2 * q + i
            for j in range(COLS):
                lanes = pl.ds(j * LANES, LANES)
                for v in range(2):
                    for t in range(2):
                        send[q, i, pl.ds(v * 16 + t * 8, 8), lanes] = grad[
                            j, pl.ds(256 * t + 16 * v + lon, 8, stride=32), :
                        ]
                send_rest[q, pl.ds(4 * i, 4), lanes] = grad[j, pl.ds(512 + lon, 4, stride=16), :]
        return 0

    lax.fori_loop(0, 8, gather, 0)
    seam, stop_here = False, False
    for at_seam, _, _ in stops(0):
        seam = jnp.logical_or(seam, at_seam)
    for d in STOPS:
        for _, at_stop, _ in stops(d):
            stop_here = jnp.logical_or(stop_here, at_stop)

    @pl.when(seam)
    def _():
        pl.semaphore_wait(barrier, len(PEERS) + 2 + len(STOPS))

    @pl.when(stop_here)
    def _():
        pl.semaphore_wait(barrier, len(PEERS) + 3)

    @pl.when(jnp.logical_not(jnp.logical_or(seam, stop_here)))
    def _():
        pl.semaphore_wait(barrier, len(PEERS) + 2)

    def to(q, source, target, sems, at):
        return pltpu.make_async_remote_copy(
            source, target, sems[0].at[at], sems[1].at[at], device_id={"lev": q}, device_id_type=MESH
        )

    go = [[], [], []]
    for part in (2, 0, 1):
        for k, q in enumerate(peers):
            if part < 2:
                copy = to(q, send.at[q, part], got.at[part, me], (go_send, go_recv), (part, k))
            else:
                copy = to(q, send_rest.at[q], got_rest.at[me], (go_send, go_recv), (part, k))
            copy.start()
            go[part].append(copy)
    own = [
        pltpu.make_async_copy(send.at[me, 0], got.at[0, me], own_sem.at[0]),
        pltpu.make_async_copy(send.at[me, 1], got.at[1, me], own_sem.at[1]),
        pltpu.make_async_copy(send_rest.at[me], got_rest.at[me], own_sem.at[2]),
    ]
    for copy in own:
        copy.start()

    row = lax.broadcasted_iota(jnp.int32, (LAT, LAT), 0)
    column = lax.broadcasted_iota(jnp.int32, (LAT, LAT), 1)
    order[...] = (row == COLS * (column & 127) + (column >> 7)).astype(F32).astype(BF16)
    back_order[...] = (column == COLS * (row & 127) + (row >> 7)).astype(F32).astype(BF16)

    for copy in loads[COLS:]:
        copy.wait()

    def coefficients(pair, _):
        for i in range(2):
            lon = 2 * pair + i
            for j in range(COLS):
                lanes = pl.ds(j * LANES, LANES)
                for t in range(2):
                    rows = pl.ds(128 * t + lon, 8, stride=16)
                    coef[t, lon, :, lanes] = sea[j, rows, :].astype(F32) * rough[j, rows, :]
                for level in range(2):
                    rows = pl.ds(256 + 16 * level + lon, 1)
                    value = sea[j, rows, :].astype(F32) * rough[j, rows, :]
                    coef_pairs[pair, pl.ds(4 * i + 2 * level, 2), lanes] = jnp.broadcast_to(
                        value, (2, LANES)
                    )
        return 0

    lax.fori_loop(0, 8, coefficients, 0)
    for t in range(2):
        value = permuted(coef[t].reshape(LON * 8, LAT), order[...]).reshape(LON, 8, LAT)
        coef[t] = value
        square[t, HALO : HALO + LON] = value * value
    value = permuted(coef_pairs[...].reshape(64, LAT), order[...]).reshape(8, 8, LAT)
    coef_pairs[...] = value
    square_pairs[HALO // 2 : HALO // 2 + 8] = value * value

    def edges(ref, span, width, sems, at):
        copies = []
        for n, (target, source, landing) in enumerate(
            ((right, span, 0), (left, width, width + span))
        ):
            copies.append(
                pltpu.make_async_remote_copy(
                    ref.at[pl.ds(source, width)], ref.at[pl.ds(landing, width)],
                    sems[0].at[at, n], sems[1].at[at, n],
                    device_id={"tile": target}, device_id_type=MESH,
                )
            )
        return copies

    def launch(ref, span, width, sems, at, d, kind, buffer):
        copies = edges(ref, span, width, sems, at)
        if d == 0:
            for copy in copies:
                copy.start()
            return
        for n, (at_seam, _, way) in enumerate(stops(d)):

            @pl.when(jnp.logical_not(at_seam))
            def _():
                copies[n].start()

            @pl.when(at_seam)
            def _():
                pltpu.make_async_remote_copy(
                    ref.at[pl.ds((span, width)[n], width)], buffer.at[pl.ds(0, width)],
                    sems[0].at[at, n], stop_recv.at[kind],
                    device_id={"tile": around(-2 * d * way)}, device_id_type=MESH,
                ).start()

    def onward(ref, span, width, sems, at, d, kind, buffer):
        return [
            (
                at_stop,
                pltpu.make_async_remote_copy(
                    buffer.at[pl.ds(0, width)], buffer.at[pl.ds(0, width)],
                    stop_send.at[kind], stop_recv.at[kind],
                    device_id={"tile": around((2 * d + 1) * way)}, device_id_type=MESH,
                ),
                pltpu.make_async_remote_copy(
                    buffer.at[pl.ds(0, width)], ref.at[pl.ds((0, width + span)[n], width)],
                    stop_send.at[kind], sems[1].at[at, n],
                    device_id={"tile": around((2 * d + 1) * way)}, device_id_type=MESH,
                ),
            )
            for n, (_, at_stop, way) in enumerate(stops(d))
        ]

    def pass_on(item):
        for at_stop, taken, copy in onward(*item):

            @pl.when(at_stop)
            def _():
                taken.wait_recv()
                copy.start()

    def passed_on(item):
        for at_stop, _, copy in onward(*item):

            @pl.when(at_stop)
            def _():
                copy.wait_send()

    coef_sems = (coef_send, coef_recv)
    coef_items = [
        (square.at[t], LON, HALO, coef_sems, t, COEF_STOPS[t], 0, stop_coef) for t in range(2)
    ]
    coef_items.append((square_pairs, LON // 2, HALO // 2, coef_sems, 2, COEF_STOPS[2], 0, stop_coef))
    for item in coef_items:
        launch(*item)

    for copy in small:
        copy.wait()
    picked = jnp.zeros((PASSES, LEVELS), F32)
    for n in range(NSCALE):
        picked = jnp.where(index[...] == n, table[n], picked)
    column = lax.broadcasted_iota(jnp.int32, (8, LEVELS), 1) - OWN * me
    row = lax.broadcasted_iota(jnp.int32, (8, LEVELS), 0)
    for t, level in enumerate((row, row + 8, 16 + ((row >> 1) & 1))):
        for p in range(PASSES):
            chosen = jnp.where(column == level, jnp.broadcast_to(picked[p : p + 1], (8, LEVELS)), 0.0)
            rates[t, p] = jnp.broadcast_to(jnp.sum(chosen, axis=1, keepdims=True), (8, LANES))

    natural[...] = jnp.zeros((512, 512), F32)
    natural[0:LEVELS, 0:LEVELS] = corr_a[...]
    natural[256 : 256 + LEVELS, 0:LEVELS] = jnp.dot(
        balance[...], corr_a[...], precision=lax.Precision.HIGHEST, preferred_element_type=F32
    )
    natural[256 : 256 + LEVELS, 256 : 256 + LEVELS] = corr_b[...]
    for i in range(2):
        half_way = exact_nt(out_rows(i), natural[...])
        full = exact_nt(half_way, in_rows(i))
        high, low = split(full[:, :256])
        weights[i, :, 0:256] = high
        weights[i, :, 256:512] = high
        weights[i, :, 512:768] = low
        tail = full[:, 256:]
        high = tail.astype(BF16).astype(F32)
        at = lax.broadcasted_iota(jnp.int32, (320, 192), 1)
        weights[i, :, 768:960] = jnp.where(at < 128, high, tail - high).astype(BF16)

    for n in range(3):
        if COEF_STOPS[n]:
            pass_on(coef_items[n])

    def take(x, places):
        high, low = split(x)
        high, low = moved(high, order[...]).astype(BF16), moved(low, order[...]).astype(BF16)
        count = x.shape[0]
        for i, start in places:
            operand[i, start : start + count, :] = high
            operand[i, start + count : start + 2 * count, :] = low
            operand[i, start + 2 * count : start + 3 * count, :] = high

    own[2].wait()
    for copy in go[2]:
        copy.wait_recv()
    take(got_rest[...].reshape(64, LAT), ((0, 768), (1, 768)))
    for i in range(2):
        own[i].wait()
        for copy in go[i]:
            copy.wait_recv()
        take(got[i].reshape(256, LAT), ((i, 0),))

    back_sems = (back_send, back_recv)

    def back(n):
        if n < 4:
            source, target = mix.at[n], land.at[n, pl.ds(2 * me, 2)]
        else:
            source, target = mix_rest, land_rest.at[me]
        remote = [to(q, source.at[q], target, back_sems, (n, k)) for k, q in enumerate(peers)]
        return remote, pltpu.make_async_copy(source.at[me], target, own_sem.at[3 + n])

    def start_back(n):
        remote, local = back(n)
        for copy in remote:
            copy.start()
        local.start()

    for t in range(2):
        for i in range(2):
            mixed = jnp.dot(
                weights[i, 128 * t : 128 * (t + 1), :], operand[i], preferred_element_type=F32
            )
            mix[2 * t : 2 * t + 2, :, i] = mixed.reshape(2, 8, 8, LAT)
        start_back(2 * t)
        start_back(2 * t + 1)
    mixed = jnp.dot(weights[0, 256:320, :], operand[0], preferred_element_type=F32)
    mixed = mixed + jnp.dot(weights[1, 256:320, :], operand[1], preferred_element_type=F32)
    mix_rest[...] = mixed.reshape(8, 8, LAT)
    start_back(4)

    edge_sems = (edge_send, edge_recv)

    def side_item(n):
        if n < 4:
            return (wave.at[n], LON, HALO, edge_sems, n, FIELD_STOPS[n], 1, stop)
        return (wave_pairs, LON // 2, HALO // 2, edge_sems, n, FIELD_STOPS[n], 1, stop)

    def arrive(n):
        remote, local = back(n)
        local.wait()
        for copy in remote:
            copy.wait_recv()
        if n < 4:
            wave[n, HALO : HALO + LON] = land[n] * coef[n // 2]
        else:
            wave_pairs[HALO // 2 : HALO // 2 + 8] = land_rest[...] * coef_pairs[...]
        launch(*side_item(n))
        if FIELD_STOPS[n]:
            pass_on(side_item(n))

    def store(rows, count, at):
        return [
            pltpu.make_async_copy(
                result.at[j, pl.ds(rows, count)],
                out_hbm.at[pl.ds(rows, count), pl.ds(j * LANES, LANES)],
                store_sem.at[at, j],
            )
            for j in range(COLS)
        ]

    def unweighted(value, c, mixed, count):
        value = jnp.where(c == 0.0, mixed, value / jnp.where(c == 0.0, 1.0, c)).reshape(count, LAT)
        high, low = split(value)
        return moved(high, back_order[...]) + moved(low, back_order[...])

    arrive(0)
    arrive(1)
    for item in coef_items:
        for copy in edges(*item[:5]):
            copy.wait()
    unpack(square_pairs, square.at[2])

    def plane(n, _):
        for k in range(5):

            @pl.when(n == k)
            def _():
                if k < 3:
                    arrive(k + 2)
                for copy in edges(*side_item(k)[:5]):
                    copy.wait()
                if k == 4:
                    unpack(wave_pairs, wave.at[4])

        diffuse(wave.at[n], square.at[n // 2], rates.at[n // 2])

        @pl.when(n < 4)
        def _():
            t, v = n // 2, n % 2
            value = unweighted(wave[n, HALO : HALO + LON], coef[t], land[n], LON * 8)
            for lon in range(LON):
                for j in range(COLS):
                    result[j, pl.ds(256 * t + 16 * v + lon, 8, stride=32), :] = value[
                        8 * lon : 8 * lon + 8, j * LANES : (j + 1) * LANES
                    ]

        for t in range(2):

            @pl.when(n == 2 * t + 1)
            def _():
                for copy in store(256 * t, 256, t):
                    copy.start()

        return 0

    lax.fori_loop(0, 5, plane, 0)

    top = lax.broadcasted_iota(jnp.int32, (8, LAT), 0) < 4
    packed = [
        jnp.where(top, wave[4, HALO + 2 * p], pltpu.roll(wave[4, HALO + 2 * p + 1], 4, 0))[None]
        for p in range(8)
    ]
    value = unweighted(jnp.concatenate(packed, 0), coef_pairs[...], land_rest[...], 64)
    for lon in range(LON):
        for j in range(COLS):
            result[j, pl.ds(512 + lon, 4, stride=16), :] = value[
                4 * lon : 4 * lon + 4, j * LANES : (j + 1) * LANES
            ]
    for copy in store(512, 64, 2):
        copy.start()
    for copies in go:
        for copy in copies:
            copy.wait_send()
    for n in range(5):
        for copy in back(n)[0]:
            copy.wait_send()
    for n in range(3):
        if COEF_STOPS[n]:
            passed_on(coef_items[n])
    for n in range(5):
        if FIELD_STOPS[n]:
            passed_on(side_item(n))
    for at, (rows, count) in enumerate(((0, 256), (256, 256), (512, 64))):
        for copy in store(rows, count, at):
            copy.wait()


def on_device(gradient, land_sea, roughness, scale_index, scale_table, balance, corr_a, corr_b):
    hbm = pl.BlockSpec(memory_space=pl.ANY)
    vmem, dma = pltpu.VMEM, pltpu.SemaphoreType.DMA
    out = pl.pallas_call(
        kernel,
        out_shape=jax.ShapeDtypeStruct((OWN * 2 * LON, LAT), F32),
        in_specs=[hbm] * 8,
        out_specs=hbm,
        scratch_shapes=[
            vmem((COLS, OWN * 2 * LON, LANES), F32),
            vmem((COLS, OWN * LON, LANES), jnp.int32),
            vmem((COLS, OWN * LON, LANES), F32),
            vmem((PASSES, LEVELS), jnp.int32),
            pltpu.SMEM((NSCALE,), F32),
            vmem((LEVELS, LEVELS), F32),
            vmem((LEVELS, LEVELS), F32),
            vmem((LEVELS, LEVELS), F32),
            vmem((8, 2, 32, LAT), F32),
            vmem((8, 8, LAT), F32),
            vmem((2, 8, 32, LAT), F32),
            vmem((8, 8, LAT), F32),
            vmem((4, 8, 2, 8, LAT), F32),
            vmem((8, 8, LAT), F32),
            vmem((4, LON, 8, LAT), F32),
            vmem((8, 8, LAT), F32),
            vmem((5, ROWS, 8, LAT), F32),
            vmem((ROWS // 2, 8, LAT), F32),
            vmem((2, LON, 8, LAT), F32),
            vmem((8, 8, LAT), F32),
            vmem((3, ROWS, 8, LAT), F32),
            vmem((ROWS // 2, 8, LAT), F32),
            vmem((3, PASSES, 8, LANES), F32),
            vmem((512, 512), F32),
            vmem((2, 320, 960), BF16),
            vmem((2, 960, LAT), BF16),
            vmem((LAT, LAT), BF16),
            vmem((LAT, LAT), BF16),
            vmem((COLS, OWN * 2 * LON, LANES), F32),
            vmem((HALO, 8, LAT), F32),
            vmem((HALO, 8, LAT), F32),
            dma((3, COLS)),
            dma((5,)),
            dma((8,)),
            dma((3, COLS)),
            dma((3, 7)),
            dma((3, 7)),
            dma((5, 7)),
            dma((5, 7)),
            dma((5, 2)),
            dma((5, 2)),
            dma((3, 2)),
            dma((3, 2)),
            dma((2,)),
            dma((2,)),
        ],
        compiler_params=pltpu.CompilerParams(
            collective_id=0, has_side_effects=True, vmem_limit_bytes=56 * 2**20
        ),
    )(
        gradient.reshape(OWN * 2 * LON, LAT),
        land_sea.reshape(OWN * LON, LAT),
        roughness.reshape(OWN * LON, LAT),
        scale_index,
        scale_table,
        balance,
        corr_a,
        corr_b,
    )
    return out.reshape(OWN, 2, LON, LAT)


def solution(mesh):
    return jax.shard_map(
        on_device,
        mesh=mesh,
        in_specs=(
            P("lev", None, "tile", None),
            P("lev", "tile", None),
            P("lev", "tile", None),
            P(),
            P(),
            P(),
            P(),
            P(),
        ),
        out_specs=P("lev", None, "tile", None),
        check_vma=False,
    )
```
